256 devices in a mesh: section: 64 (over x_lo, z, y), sp: 4 (over x_hi, core).
Axes of the slice: x: 4 (x_hi: 2, x_lo: 2; x = x_hi * 2 + x_lo), y: 4, z: 8, core: 2. Of those that a mesh axis runs over, the one named last changes fastest.
Arguments:
- patches: bfloat16 [64, 256, 3072], P('section', 'sp'), may hold values from -6 to 6
- patch_ids: int32 [64], P('section'), may hold values from 0 to 5
- step_ids: int32 [64], P('section'), may hold values from 0 to 27
- modulation: bfloat16 [64, 28, 9216], P('section'), may hold values from -3 to 3
- w_qkv: bfloat16 [64, 3, 3072, 1536], P('section', None, None, 'sp'), may hold values from -0.109375 to 0.109375
- w_out: bfloat16 [64, 1536, 3072], P('section', 'sp'), may hold values from -0.15625 to 0.15625
- gains: float32 [64, 2, 128], P('section'), may hold values from 1.2 to 2.5
- stale_keys: bfloat16 [64, 1536, 1536], P('section', None, 'sp'), may hold values from -9 to 9
- stale_values: bfloat16 [64, 1536, 1536], P('section', None, 'sp'), may hold values from -6 to 6
Outputs:
- handed: bfloat16 [64, 256, 3072], P('section', 'sp')
The draws below stay inside these ranges and needn't reach their ends.
All inputs are finite; a program needn't handle non-finite values.
Results may differ from the reference program's by a relative error of at most 0.0065.
Values may be sent and summed in bfloat16 or wider, within the bound.
No kernel may reach another device: no remote copies, remote signals or barrier semaphores. Data moves between devices by JAX's collectives and lax.ppermute only.
A program may use at most 128 MiB of HBM per device.

```python
import math
import jax
import jax.numpy as jnp
from jax import lax

D = 3072
H = 12
HD = 128
PT = 256
PATCHES = 6
STEPS = 28
S = 1536
N_SECTION = 64


def set_ends(values, rng, least, top_value):
    longest = values.shape.index(max(values.shape))
    spots = []
    for shift in (0, 1):
        where = [jax.random.randint(jax.random.fold_in(rng, axis), (), 0, length) for axis, length in enumerate(values.shape)]
        where[longest] = (where[longest] + shift) % values.shape[longest]
        spots.append(tuple(where))
    return values.at[spots[0]].set(least).at[spots[1]].set(top_value)


def block_levels(stream_key, shape, cuts, smallest, top_value):
    factor_of = 1.0
    for dim, parts in cuts:
        heights = jax.random.uniform(jax.random.fold_in(jax.random.fold_in(stream_key, 6), dim), (parts,), jnp.float32, smallest / len(cuts), top_value / len(cuts))
        factor_of = factor_of * jnp.repeat(jnp.exp(heights), shape[dim] // parts).reshape((-1,) + (1,) * (len(shape) - 1 - dim))
    return factor_of


def noise(key, shape, spread, bound, pieces=(), held_as=jnp.bfloat16):
    array = jax.random.normal(key, shape, jnp.float32) * spread
    if len(pieces) > 0:
        array = block_levels(key, shape, pieces, -0.22, 0.18) * array
    return jnp.clip(array, min=-bound, max=bound).astype(held_as)


def setup_inputs(seed: int = 0) -> dict:
    splits = jax.random.split(jax.random.key(seed), 10)
    patches = noise(splits[0], (N_SECTION, PT, D), 1.0, 6.0, ((0, 64), (1, 4)))
    patch_ids = set_ends(jax.random.randint(splits[1], (N_SECTION,), 0, PATCHES), jax.random.fold_in(splits[1], 1), 0, PATCHES - 1).astype(jnp.int32)
    step_ids = set_ends(jax.random.randint(splits[2], (N_SECTION,), 0, STEPS), jax.random.fold_in(splits[2], 1), 0, STEPS - 1).astype(jnp.int32)
    modulation = noise(splits[3], (N_SECTION, STEPS, 3 * D), 0.5, 3.0, ((0, 64),))
    w_qkv = noise(splits[4], (N_SECTION, 3, D, H * HD), D ** -0.5, 0.109375, ((0, 64), (3, 4)))
    w_out = noise(splits[5], (N_SECTION, H * HD, D), (H * HD) ** -0.5, 0.15625, ((0, 64), (1, 4)))
    gains = jnp.clip(jnp.exp(math.log(2.5) - 0.73396914 * jax.random.uniform(splits[6], (N_SECTION, 2, HD), jnp.float32) ** block_levels(splits[6], (N_SECTION, 2, HD), ((0, 64),), -0.2, 0.2)), 1.2, 2.5)
    stale_keys = noise(splits[7], (N_SECTION, S, H * HD), 1.5, 9.0, ((0, 64), (2, 4)))
    stale_values = noise(splits[8], (N_SECTION, S, H * HD), 1.0, 6.0, ((0, 64), (2, 4)))
    return {"patches": patches, "patch_ids": patch_ids, "step_ids": step_ids, "modulation": modulation, "w_qkv": w_qkv, "w_out": w_out, "gains": gains, "stale_keys": stale_keys, "stale_values": stale_values}


def head_norm(values, gains):
    shaped = values.reshape(values.shape[0], H, HD)
    square = lax.optimization_barrier(jnp.mean(shaped * shaped, axis=-1, keepdims=True))
    shaped = shaped * lax.rsqrt(square + 1e-06) * gains
    return shaped.reshape(values.shape[0], H * HD).astype(jnp.bfloat16)

def section_block(operands):
    patch, weights_qkv, weights_out, modulation, norm_gains, old_keys, old_values, patch_index, step_index = operands
    stream = patch.astype(jnp.float32)
    row_mean = lax.optimization_barrier(jnp.mean(stream, axis=-1, keepdims=True))
    centred = stream - row_mean
    row_var = lax.optimization_barrier(jnp.mean(centred * centred, axis=-1, keepdims=True))
    mod_row = lax.dynamic_index_in_dim(modulation, step_index, 0, keepdims=False).astype(jnp.float32)
    mod_shift = mod_row[:D]
    mod_scale = mod_row[D:2 * D]
    mod_gate = mod_row[2 * D:]
    normed = (centred * lax.rsqrt(row_var + 1e-06) * (1.0 + mod_scale) + mod_shift).astype(jnp.bfloat16)
    queries = head_norm(jnp.dot(normed, weights_qkv[0], preferred_element_type=jnp.float32), norm_gains[0])
    fresh_keys = head_norm(jnp.dot(normed, weights_qkv[1], preferred_element_type=jnp.float32), norm_gains[1])
    fresh_values = jnp.dot(normed, weights_qkv[2], preferred_element_type=jnp.float32).astype(jnp.bfloat16)
    first_row = (patch_index * PT).astype(jnp.int32)
    zero_col = jnp.zeros((), jnp.int32)
    all_keys = lax.dynamic_update_slice(old_keys, fresh_keys, (first_row, zero_col))
    all_values = lax.dynamic_update_slice(old_values, fresh_values, (first_row, zero_col))
    query_heads = queries.reshape(PT, H, HD).astype(jnp.float32)
    key_heads = all_keys.reshape(S, H, HD).astype(jnp.float32)
    value_heads = all_values.reshape(S, H, HD).astype(jnp.float32)
    scores = jnp.einsum('phd,shd->hps', query_heads, key_heads) * (1.0 / HD ** 0.5)
    weights = jax.nn.softmax(scores, axis=-1).astype(jnp.bfloat16)
    attended = jnp.einsum('hps,shd->phd', weights.astype(jnp.float32), value_heads)
    attended = attended.reshape(PT, H * HD).astype(jnp.bfloat16)
    projected = jnp.dot(attended, weights_out, preferred_element_type=jnp.float32)
    return (stream + mod_gate * projected).astype(jnp.bfloat16)

def reference(patches, patch_ids, step_ids, modulation, w_qkv, w_out, gains, stale_keys, stale_values):
    produced = lax.map(section_block, (patches, w_qkv, w_out, modulation, gains, stale_keys, stale_values, patch_ids, step_ids))
    return jnp.roll(produced, 1, axis=0)
```

```python
import functools

import jax
import jax.numpy as jnp
from jax import lax
from jax.experimental import pallas as pl
from jax.experimental.pallas import tpu as pltpu
from jax.sharding import PartitionSpec as P

CHUNKS = 4
F32 = jnp.float32
BF16 = jnp.bfloat16
VMEM = pl.BlockSpec(memory_space=pltpu.VMEM)
HBM = pl.BlockSpec(memory_space=pltpu.HBM)
SMEM = pl.BlockSpec(memory_space=pltpu.SMEM)


def params(mib=24):
    return pltpu.CompilerParams(vmem_limit_bytes=int(mib * 1024) * 1024)


def cost(flops, data):
    return pl.CostEstimate(flops=int(flops), bytes_accessed=int(data), transcendentals=0)


def in_hbm(block):
    return pltpu.with_memory_space_constraint(block, pltpu.HBM)


def swapped(block, flip):
    return lax.ppermute(block, "sp", [(i, i ^ flip) for i in range(lax.axis_size("sp"))])


def shifted(block):
    sections = lax.axis_size("section")
    return lax.ppermute(block, "section", [(i, (i + 1) % sections) for i in range(sections)])


def modulated(block, mod):
    width = block.shape[1]
    stream = block.astype(F32)
    mean = jnp.sum(stream, axis=-1, keepdims=True) * (1.0 / width)
    centred = stream - mean
    var = jnp.sum(centred * centred, axis=-1, keepdims=True) * (1.0 / width)
    return (centred * lax.rsqrt(var + 1e-06) * (1.0 + mod[1:2]) + mod[0:1]).astype(BF16)


def head_norm(values, gain):
    size = gain.shape[1]
    heads = []
    for h in range(values.shape[1] // size):
        head = values[:, h * size : (h + 1) * size]
        square = jnp.sum(head * head, axis=-1, keepdims=True) * (1.0 / size)
        heads.append((head * lax.rsqrt(square + 1e-06) * gain).astype(BF16))
    return jnp.concatenate(heads, axis=1)


def qkv(normed, w_ref, gains_ref):
    q = jnp.dot(normed, w_ref[0], preferred_element_type=F32)
    k = jnp.dot(normed, w_ref[1], preferred_element_type=F32)
    v = jnp.dot(normed, w_ref[2], preferred_element_type=F32)
    return head_norm(q, gains_ref[0:1]), head_norm(k, gains_ref[1:2]), v.astype(BF16)


def attend(q, kt_ref, v_ref, size):
    scale = 1.0 / size**0.5
    heads = []
    for h in range(q.shape[1] // size):
        cols = slice(h * size, (h + 1) * size)
        scores = jnp.dot(q[:, cols], kt_ref[cols, :], preferred_element_type=F32)
        top = jnp.max(scores, axis=-1, keepdims=True)
        weights = jnp.exp((scores - top) * scale)
        total = jnp.sum(weights, axis=-1, keepdims=True)
        out = jnp.dot(weights.astype(BF16), v_ref[:, cols], preferred_element_type=F32)
        heads.append((out / total).astype(BF16))
    return jnp.concatenate(heads, axis=1)


def near_kernel(
    pid_ref, own_hbm, mate_ref, mod_ref, gains_hbm, w_hbm, sk_hbm, sv_hbm,
    q_ref, kt_ref, v_ref, w_ref, acc_ref, stat_ref,
    xn, own_ref, gains_ref, sk_ref, sems,
):
    rows = own_ref.shape[0]
    size = gains_ref.shape[1]
    heads = q_ref.shape[1] // size
    early = [
        pltpu.make_async_copy(own_hbm, own_ref, sems.at[5]),
        pltpu.make_async_copy(gains_hbm, gains_ref, sems.at[6]),
    ]
    for load in early:
        load.start()
    loads = [pltpu.make_async_copy(w_hbm.at[i], w_ref.at[i], sems.at[i]) for i in range(3)]
    loads.append(pltpu.make_async_copy(sk_hbm, sk_ref, sems.at[3]))
    loads.append(pltpu.make_async_copy(sv_hbm, v_ref, sems.at[4]))
    loads[3].start()
    loads[0].start()
    loads[1].start()
    xn[rows:] = modulated(mate_ref[...], mod_ref)
    for load in early:
        load.wait()
    xn[:rows] = modulated(own_ref[...], mod_ref)
    first = pl.multiple_of(pid_ref[0] * (4 * rows), 4 * rows)
    loads[3].wait()
    kt_ref[...] = sk_ref[...].T
    loads[0].wait()
    loads[2].start()
    loads[4].start()
    q = head_norm(jnp.dot(xn[...], w_ref[0], preferred_element_type=F32), gains_ref[0:1])
    q_ref[...] = q
    loads[1].wait()
    k = head_norm(jnp.dot(xn[...], w_ref[1], preferred_element_type=F32), gains_ref[1:2])
    kt_ref[:, pl.ds(first, 2 * rows)] = k.T
    loads[2].wait()
    v = jnp.dot(xn[...], w_ref[2], preferred_element_type=F32).astype(BF16)
    loads[4].wait()
    v_ref[pl.ds(first, 2 * rows)] = v
    place = lax.broadcasted_iota(jnp.int32, (1, kt_ref.shape[1]), 1) - (first + 2 * rows)
    bias = jnp.where((place >= 0) & (place < 2 * rows), -1e30, 0.0)
    scale = 1.0 / size**0.5
    for h in range(heads):
        cols = slice(h * size, (h + 1) * size)
        scores = jnp.dot(q[:, cols], kt_ref[cols, :], preferred_element_type=F32) + bias
        top = jnp.max(scores, axis=-1, keepdims=True)
        weights = jnp.exp((scores - top) * scale)
        stat_ref[:, h : h + 1] = top
        stat_ref[:, heads + h : heads + h + 1] = jnp.sum(weights, axis=-1, keepdims=True)
        acc_ref[:, cols] = jnp.dot(weights.astype(BF16), v_ref[:, cols], preferred_element_type=F32)


def far_kernel(
    pid_ref, own_ref, mate_ref, mod_ref, gains_ref, w_ref, ki_ref, vi_ref, qn_ref, acc_ref, stat_ref,
    q_ref, mine_ref, send_ref, kt_ref, v_ref, xn,
):
    rows = own_ref.shape[0]
    size = gains_ref.shape[1]
    heads = q_ref.shape[1] // size
    scale = 1.0 / size**0.5
    xn[:rows] = modulated(own_ref[...], mod_ref)
    xn[rows:] = modulated(mate_ref[...], mod_ref)
    q, k, v = qkv(xn[...], w_ref, gains_ref)
    first = pl.multiple_of(pid_ref[0] * (4 * rows), 4 * rows) + 2 * rows
    first = pl.multiple_of(first, 2 * rows)
    fresh = k.T
    kt_ref[:, pl.ds(first, 2 * rows)] = fresh
    v_ref[pl.ds(first, 2 * rows)] = v
    q_ref[...] = q[:rows]
    for h in range(heads):
        cols = slice(h * size, (h + 1) * size)
        scores = jnp.dot(qn_ref[:, cols], fresh[cols, :], preferred_element_type=F32)
        before = stat_ref[:, h : h + 1]
        top = jnp.maximum(before, jnp.max(scores, axis=-1, keepdims=True))
        weights = jnp.exp((scores - top) * scale)
        keep = jnp.exp((before - top) * scale)
        total = stat_ref[:, heads + h : heads + h + 1] * keep + jnp.sum(weights, axis=-1, keepdims=True)
        out = acc_ref[:, cols] * keep + jnp.dot(weights.astype(BF16), v[:, cols], preferred_element_type=F32)
        out = (out / total).astype(BF16)
        mine_ref[:, cols] = out[:rows]
        send_ref[:rows, cols] = out[rows:]
    send_ref[rows:] = attend(q[rows:], kt_ref, v_ref, size)


def mine_kernel(q_ref, kt_ref, v_ref, mine_ref, *, size):
    mine_ref[...] = attend(q_ref[...], kt_ref, v_ref, size)


def projected(mine_ref, recv, w_ref, wm_ref, cols):
    part = jnp.dot(mine_ref[...], w_ref[:, cols], preferred_element_type=F32)
    return part + jnp.dot(recv, wm_ref[:, cols], preferred_element_type=F32)


def far_out_kernel(mine_ref, recv_ref, w_ref, wm_ref, *out_refs):
    rows, width = out_refs[0].shape
    for c, out in enumerate(out_refs):
        cols = slice(c * width, (c + 1) * width)
        out[...] = projected(mine_ref, recv_ref[rows:], w_ref, wm_ref, cols).astype(BF16)


def own_out_kernel(mine_ref, recv_ref, w_ref, wm_ref, stream_ref, mod_ref, *out_refs):
    rows, width = out_refs[0].shape
    for c, out in enumerate(out_refs):
        cols = slice(c * width, (c + 1) * width)
        part = projected(mine_ref, recv_ref[:rows], w_ref, wm_ref, cols)
        out[...] = stream_ref[:, cols].astype(F32) + mod_ref[2:3, cols] * part


def final_kernel(acc_ref, far_ref, mod_ref, out_ref, *, start):
    gate = mod_ref[2:3, start : start + out_ref.shape[1]]
    out_ref[...] = (acc_ref[...] + gate * far_ref[...].astype(F32)).astype(BF16)


def first_kernel(part_ref, out_hbm, sem):
    copy = pltpu.make_async_copy(part_ref, out_hbm.at[0, :, pl.ds(0, part_ref.shape[1])], sem)
    copy.start()
    copy.wait()


def next_kernel(part_ref, held_hbm, out_hbm, sem, *, start):
    copy = pltpu.make_async_copy(part_ref, out_hbm.at[0, :, pl.ds(start, part_ref.shape[1])], sem)
    copy.start()
    copy.wait()


def shape(*dims, dtype=BF16):
    return jax.ShapeDtypeStruct(dims, dtype)


def body(patches, patch_ids, step_ids, modulation, w_qkv, w_out, gains, stale_keys, stale_values):
    rows, width = patches.shape[1:]
    size = gains.shape[2]
    cols = stale_keys.shape[2]
    keys = stale_keys.shape[1]
    own = patches[0]
    x_far = swapped(own, 2)
    x_mate = swapped(own, 1)
    w_mate = swapped(w_out[0], 1)
    mod = lax.dynamic_index_in_dim(modulation[0], step_ids[0], 0, keepdims=False)
    mod = mod.reshape(3, width).astype(F32)
    half_flops = 2 * 2 * rows * width * 3 * cols
    att_flops = 2 * 2 * rows * keys * cols
    q_own, k_part, v_part, w_held, acc, stat = pl.pallas_call(
        near_kernel,
        out_shape=[
            pltpu.VMEM((2 * rows, cols), BF16),
            pltpu.VMEM((cols, keys), BF16),
            pltpu.VMEM((keys, cols), BF16),
            pltpu.VMEM((3, width, cols), BF16),
            pltpu.VMEM((2 * rows, cols), F32),
            pltpu.VMEM((2 * rows, size), F32),
        ],
        in_specs=[SMEM, HBM, VMEM, VMEM, HBM, HBM, HBM, HBM],
        out_specs=[VMEM] * 6,
        scratch_shapes=[
            pltpu.VMEM((2 * rows, width), BF16),
            pltpu.VMEM((rows, width), BF16),
            pltpu.VMEM((2, size), F32),
            pltpu.VMEM((keys, cols), BF16),
            pltpu.SemaphoreType.DMA((7,)),
        ],
        compiler_params=params(),
        cost_estimate=cost(half_flops, 1),
        name="near",
    )(
        patch_ids,
        in_hbm(own),
        x_mate,
        mod,
        in_hbm(gains[0]),
        in_hbm(w_qkv[0]),
        in_hbm(stale_keys[0]),
        in_hbm(stale_values[0]),
    )
    x_far, q_own = lax.optimization_barrier((x_far, q_own))
    x_far_mate = swapped(x_far, 1)
    far_q, own_mine, send, k_all, v_all = pl.pallas_call(
        far_kernel,
        out_shape=[
            pltpu.VMEM((rows, cols), BF16),
            pltpu.VMEM((rows, cols), BF16),
            pltpu.VMEM((2 * rows, cols), BF16),
            pltpu.VMEM((cols, keys), BF16),
            pltpu.VMEM((keys, cols), BF16),
        ],
        in_specs=[SMEM] + [VMEM] * 10,
        out_specs=[VMEM] * 5,
        input_output_aliases={6: 3, 7: 4},
        scratch_shapes=[pltpu.VMEM((2 * rows, width), BF16)],
        compiler_params=params(),
        cost_estimate=cost(half_flops + att_flops, 12e6),
        name="far",
    )(patch_ids, x_far, x_far_mate, mod, gains[0], w_held, k_part, v_part, q_own, acc, stat)
    recv = swapped(send, 1)
    far_mine = pl.pallas_call(
        functools.partial(mine_kernel, size=size),
        out_shape=pltpu.VMEM((rows, cols), BF16),
        in_specs=[VMEM] * 3,
        out_specs=VMEM,
        compiler_params=params(),
        cost_estimate=cost(att_flops, 3e6),
        name="far_mine",
    )(far_q, k_all, v_all)
    recv, far_mine = lax.optimization_barrier((recv, far_mine))
    step = width // CHUNKS
    far_parts = pl.pallas_call(
        far_out_kernel,
        out_shape=[pltpu.VMEM((rows, step), BF16)] * CHUNKS,
        in_specs=[VMEM] * 4,
        out_specs=[VMEM] * CHUNKS,
        compiler_params=params(),
        cost_estimate=cost(2 * rows * 2 * cols * width, 5e6),
        name="far_out",
    )(far_mine, recv, w_out[0], w_mate)
    far_parts, own_mine = lax.optimization_barrier((far_parts, own_mine))
    arrived = [swapped(part, 2) for part in far_parts]
    own_parts = pl.pallas_call(
        own_out_kernel,
        out_shape=[pltpu.VMEM((rows, step), F32)] * CHUNKS,
        in_specs=[VMEM] * 6,
        out_specs=[VMEM] * CHUNKS,
        compiler_params=params(),
        cost_estimate=cost(1, 1),
        name="own_out",
    )(own_mine, recv, w_out[0], w_mate, own, mod)
    handed = None
    for c in range(CHUNKS):
        produced = pl.pallas_call(
            functools.partial(final_kernel, start=c * step),
            out_shape=pltpu.VMEM((rows, step), BF16),
            in_specs=[VMEM] * 3,
            out_specs=VMEM,
            compiler_params=params(),
            cost_estimate=cost(1, 1),
            name="final",
        )(own_parts[c], arrived[c], mod)
        there = shifted(produced)
        held = [] if handed is None else [handed]
        handed = pl.pallas_call(
            functools.partial(next_kernel, start=c * step) if held else first_kernel,
            out_shape=pltpu.HBM((1, rows, width), BF16),
            in_specs=[VMEM] + [HBM] * len(held),
            out_specs=HBM,
            input_output_aliases={1: 0} if held else {},
            scratch_shapes=[pltpu.SemaphoreType.DMA],
            compiler_params=params(),
            cost_estimate=cost(1, 1),
            name="place",
        )(there, *held)
    return handed


def solution(mesh):
    return jax.shard_map(
        body,
        mesh=mesh,
        in_specs=(
            P("section", "sp", None),
            P("section"),
            P("section"),
            P("section", None, None),
            P("section", None, None, "sp"),
            P("section", "sp", None),
            P("section", None, None),
            P("section", None, "sp"),
            P("section", None, "sp"),
        ),
        out_specs=P("section", "sp", None),
        check_vma=False,
    )
```

```python
import functools

import jax
import jax.numpy as jnp
from jax import lax
from jax.experimental import pallas as pl
from jax.experimental.pallas import tpu as pltpu
from jax.sharding import PartitionSpec as P

SHARES = (6, 6, 6, 6)
F32 = jnp.float32
BF16 = jnp.bfloat16
VMEM = pl.BlockSpec(memory_space=pltpu.VMEM)
HBM = pl.BlockSpec(memory_space=pltpu.HBM)
SMEM = pl.BlockSpec(memory_space=pltpu.SMEM)


def params(mib=24):
    return pltpu.CompilerParams(vmem_limit_bytes=int(mib * 1024) * 1024)


def cost(flops, data):
    return pl.CostEstimate(flops=int(flops), bytes_accessed=int(data), transcendentals=0)


def in_hbm(block):
    return pltpu.with_memory_space_constraint(block, pltpu.HBM)


def swapped(block, flip):
    return lax.ppermute(block, "sp", [(i, i ^ flip) for i in range(lax.axis_size("sp"))])


def shifted(block):
    sections = lax.axis_size("section")
    return lax.ppermute(block, "section", [(i, (i + 1) % sections) for i in range(sections)])


def modulated(block, mod):
    width = block.shape[1]
    stream = block.astype(F32)
    mean = jnp.sum(stream, axis=-1, keepdims=True) * (1.0 / width)
    centred = stream - mean
    var = jnp.sum(centred * centred, axis=-1, keepdims=True) * (1.0 / width)
    return (centred * lax.rsqrt(var + 1e-06) * (1.0 + mod[1:2]) + mod[0:1]).astype(BF16)


def head_norm(values, gain):
    size = gain.shape[1]
    heads = []
    for h in range(values.shape[1] // size):
        head = values[:, h * size : (h + 1) * size]
        square = jnp.sum(head * head, axis=-1, keepdims=True) * (1.0 / size)
        heads.append((head * lax.rsqrt(square + 1e-06) * gain).astype(BF16))
    return jnp.concatenate(heads, axis=1)


def qkv(normed, w_ref, gains_ref):
    q = jnp.dot(normed, w_ref[0], preferred_element_type=F32)
    k = jnp.dot(normed, w_ref[1], preferred_element_type=F32)
    v = jnp.dot(normed, w_ref[2], preferred_element_type=F32)
    return head_norm(q, gains_ref[0:1]), head_norm(k, gains_ref[1:2]), v.astype(BF16)


def attend(q, kt_ref, v_ref, size):
    scale = 1.0 / size**0.5
    heads = []
    for h in range(q.shape[1] // size):
        cols = slice(h * size, (h + 1) * size)
        scores = jnp.dot(q[:, cols], kt_ref[cols, :], preferred_element_type=F32)
        top = jnp.max(scores, axis=-1, keepdims=True)
        weights = jnp.exp((scores - top) * scale)
        total = jnp.sum(weights, axis=-1, keepdims=True)
        out = jnp.dot(weights.astype(BF16), v_ref[:, cols], preferred_element_type=F32)
        heads.append((out / total).astype(BF16))
    return jnp.concatenate(heads, axis=1)


def near_kernel(
    pid_ref, own_hbm, mate_ref, mod_ref, gains_hbm, w_hbm, sk_hbm, sv_hbm, wo_hbm,
    q_ref, kt_ref, v_ref, w_ref, acc_ref, stat_ref, wo_ref,
    xn, own_ref, gains_ref, sk_ref, sems,
):
    rows = own_ref.shape[0]
    size = gains_ref.shape[1]
    heads = q_ref.shape[1] // size
    early = [
        pltpu.make_async_copy(own_hbm, own_ref, sems.at[5]),
        pltpu.make_async_copy(gains_hbm, gains_ref, sems.at[6]),
    ]
    for load in early:
        load.start()
    loads = [pltpu.make_async_copy(w_hbm.at[i], w_ref.at[i], sems.at[i]) for i in range(3)]
    loads.append(pltpu.make_async_copy(sk_hbm, sk_ref, sems.at[3]))
    loads.append(pltpu.make_async_copy(sv_hbm, v_ref, sems.at[4]))
    loads.append(pltpu.make_async_copy(wo_hbm, wo_ref, sems.at[7]))
    loads[3].start()
    loads[0].start()
    loads[1].start()
    xn[rows:] = modulated(mate_ref[...], mod_ref)
    for load in early:
        load.wait()
    xn[:rows] = modulated(own_ref[...], mod_ref)
    first = pl.multiple_of(pid_ref[0] * (4 * rows), 4 * rows)
    loads[3].wait()
    kt_ref[...] = sk_ref[...].T
    loads[0].wait()
    loads[2].start()
    loads[4].start()
    q = head_norm(jnp.dot(xn[...], w_ref[0], preferred_element_type=F32), gains_ref[0:1])
    q_ref[...] = q
    loads[1].wait()
    loads[5].start()
    k = head_norm(jnp.dot(xn[...], w_ref[1], preferred_element_type=F32), gains_ref[1:2])
    kt_ref[:, pl.ds(first, 2 * rows)] = k.T
    loads[2].wait()
    v = jnp.dot(xn[...], w_ref[2], preferred_element_type=F32).astype(BF16)
    loads[4].wait()
    v_ref[pl.ds(first, 2 * rows)] = v
    place = lax.broadcasted_iota(jnp.int32, (1, kt_ref.shape[1]), 1) - (first + 2 * rows)
    bias = jnp.where((place >= 0) & (place < 2 * rows), -1e30, 0.0)
    scale = 1.0 / size**0.5
    for h in range(heads):
        cols = slice(h * size, (h + 1) * size)
        scores = jnp.dot(q[:, cols], kt_ref[cols, :], preferred_element_type=F32) + bias
        top = jnp.max(scores, axis=-1, keepdims=True)
        weights = jnp.exp((scores - top) * scale)
        stat_ref[:, h : h + 1] = top
        stat_ref[:, heads + h : heads + h + 1] = jnp.sum(weights, axis=-1, keepdims=True)
        acc_ref[:, cols] = jnp.dot(weights.astype(BF16), v_ref[:, cols], preferred_element_type=F32)
    loads[5].wait()


def far_kernel(
    pid_ref, own_ref, mate_ref, mod_ref, gains_ref, w_ref, ki_ref, vi_ref, qn_ref, acc_ref, stat_ref,
    q_ref, mine_ref, send_ref, kt_ref, v_ref, xn,
):
    rows = own_ref.shape[0]
    size = gains_ref.shape[1]
    heads = q_ref.shape[1] // size
    scale = 1.0 / size**0.5
    xn[:rows] = modulated(own_ref[...], mod_ref)
    xn[rows:] = modulated(mate_ref[...], mod_ref)
    q, k, v = qkv(xn[...], w_ref, gains_ref)
    first = pl.multiple_of(pid_ref[0] * (4 * rows), 4 * rows) + 2 * rows
    first = pl.multiple_of(first, 2 * rows)
    fresh = k.T
    kt_ref[:, pl.ds(first, 2 * rows)] = fresh
    v_ref[pl.ds(first, 2 * rows)] = v
    q_ref[...] = q[:rows]
    for h in range(heads):
        cols = slice(h * size, (h + 1) * size)
        scores = jnp.dot(qn_ref[:, cols], fresh[cols, :], preferred_element_type=F32)
        before = stat_ref[:, h : h + 1]
        top = jnp.maximum(before, jnp.max(scores, axis=-1, keepdims=True))
        weights = jnp.exp((scores - top) * scale)
        keep = jnp.exp((before - top) * scale)
        total = stat_ref[:, heads + h : heads + h + 1] * keep + jnp.sum(weights, axis=-1, keepdims=True)
        out = acc_ref[:, cols] * keep + jnp.dot(weights.astype(BF16), v[:, cols], preferred_element_type=F32)
        out = (out / total).astype(BF16)
        mine_ref[:, cols] = out[:rows]
        send_ref[:rows, cols] = out[rows:]
    send_ref[rows:] = attend(q[rows:], kt_ref, v_ref, size)


def mine_kernel(q_ref, kt_ref, v_ref, mine_ref, *, size):
    mine_ref[...] = attend(q_ref[...], kt_ref, v_ref, size)


def projected(mine_ref, recv, w_ref, wm_ref, cols):
    part = jnp.dot(mine_ref[...], w_ref[:, cols], preferred_element_type=F32)
    return part + jnp.dot(recv, wm_ref[:, cols], preferred_element_type=F32)


def far_out_kernel(mine_ref, recv_ref, w_ref, wm_ref, *out_refs):
    rows = mine_ref.shape[0]
    start = 0
    for out in out_refs:
        cols = slice(start, start + out.shape[1])
        start = cols.stop
        out[...] = projected(mine_ref, recv_ref[rows:], w_ref, wm_ref, cols).astype(BF16)


def final_kernel(mine_ref, recv_ref, w_ref, wm_ref, stream_ref, mod_ref, far_ref, out_ref, *, start):
    rows = mine_ref.shape[0]
    cols = slice(start, start + out_ref.shape[1])
    part = projected(mine_ref, recv_ref[:rows], w_ref, wm_ref, cols) + far_ref[...].astype(F32)
    out_ref[...] = (stream_ref[:, cols].astype(F32) + mod_ref[2:3, cols] * part).astype(BF16)


def first_kernel(part_ref, out_hbm, sem):
    copy = pltpu.make_async_copy(part_ref, out_hbm.at[0, :, pl.ds(0, part_ref.shape[1])], sem)
    copy.start()
    copy.wait()


def next_kernel(part_ref, held_hbm, out_hbm, sem, *, start):
    copy = pltpu.make_async_copy(part_ref, out_hbm.at[0, :, pl.ds(start, part_ref.shape[1])], sem)
    copy.start()
    copy.wait()


def shape(*dims, dtype=BF16):
    return jax.ShapeDtypeStruct(dims, dtype)


def body(patches, patch_ids, step_ids, modulation, w_qkv, w_out, gains, stale_keys, stale_values):
    rows, width = patches.shape[1:]
    size = gains.shape[2]
    cols = stale_keys.shape[2]
    keys = stale_keys.shape[1]
    own = patches[0]
    x_far = swapped(own, 2)
    x_mate = swapped(own, 1)
    w_mate = swapped(w_out[0], 1)
    mod = lax.dynamic_index_in_dim(modulation[0], step_ids[0], 0, keepdims=False)
    mod = mod.reshape(3, width).astype(F32)
    half_flops = 2 * 2 * rows * width * 3 * cols
    att_flops = 2 * 2 * rows * keys * cols
    q_own, k_part, v_part, w_held, acc, stat, w_own = pl.pallas_call(
        near_kernel,
        out_shape=[
            pltpu.VMEM((2 * rows, cols), BF16),
            pltpu.VMEM((cols, keys), BF16),
            pltpu.VMEM((keys, cols), BF16),
            pltpu.VMEM((3, width, cols), BF16),
            pltpu.VMEM((2 * rows, cols), F32),
            pltpu.VMEM((2 * rows, size), F32),
            pltpu.VMEM((cols, width), BF16),
        ],
        in_specs=[SMEM, HBM, VMEM, VMEM] + [HBM] * 5,
        out_specs=[VMEM] * 7,
        scratch_shapes=[
            pltpu.VMEM((2 * rows, width), BF16),
            pltpu.VMEM((rows, width), BF16),
            pltpu.VMEM((2, size), F32),
            pltpu.VMEM((keys, cols), BF16),
            pltpu.SemaphoreType.DMA((8,)),
        ],
        compiler_params=params(),
        cost_estimate=cost(half_flops, 1),
        name="near",
    )(
        patch_ids,
        in_hbm(own),
        x_mate,
        mod,
        in_hbm(gains[0]),
        in_hbm(w_qkv[0]),
        in_hbm(stale_keys[0]),
        in_hbm(stale_values[0]),
        in_hbm(w_out[0]),
    )
    x_far, q_own = lax.optimization_barrier((x_far, q_own))
    x_far_mate = swapped(x_far, 1)
    far_q, own_mine, send, k_all, v_all = pl.pallas_call(
        far_kernel,
        out_shape=[
            pltpu.VMEM((rows, cols), BF16),
            pltpu.VMEM((rows, cols), BF16),
            pltpu.VMEM((2 * rows, cols), BF16),
            pltpu.VMEM((cols, keys), BF16),
            pltpu.VMEM((keys, cols), BF16),
        ],
        in_specs=[SMEM] + [VMEM] * 10,
        out_specs=[VMEM] * 5,
        input_output_aliases={6: 3, 7: 4},
        scratch_shapes=[pltpu.VMEM((2 * rows, width), BF16)],
        compiler_params=params(),
        cost_estimate=cost(half_flops + att_flops, 12e6),
        name="far",
    )(patch_ids, x_far, x_far_mate, mod, gains[0], w_held, k_part, v_part, q_own, acc, stat)
    recv = swapped(send, 1)
    far_mine = pl.pallas_call(
        functools.partial(mine_kernel, size=size),
        out_shape=pltpu.VMEM((rows, cols), BF16),
        in_specs=[VMEM] * 3,
        out_specs=VMEM,
        compiler_params=params(),
        cost_estimate=cost(att_flops, 3e6),
        name="far_mine",
    )(far_q, k_all, v_all)
    recv, far_mine = lax.optimization_barrier((recv, far_mine))
    steps = [width // sum(SHARES) * share for share in SHARES]
    starts = [sum(steps[:c]) for c in range(len(steps))]
    far_parts = pl.pallas_call(
        far_out_kernel,
        out_shape=[pltpu.VMEM((rows, step), BF16) for step in steps],
        in_specs=[VMEM] * 4,
        out_specs=[VMEM] * len(steps),
        compiler_params=params(),
        cost_estimate=cost(2 * rows * 2 * cols * width, 5e6),
        name="far_out",
    )(far_mine, recv, w_own, w_mate)
    far_parts, own_mine = lax.optimization_barrier((far_parts, own_mine))
    arrived = [swapped(part, 2) for part in far_parts]
    handed = produced = None
    for c, step in enumerate(steps):
        if c > 0:
            arrived[c], produced = lax.optimization_barrier((arrived[c], produced))
        produced = pl.pallas_call(
            functools.partial(final_kernel, start=starts[c]),
            out_shape=pltpu.VMEM((rows, step), BF16),
            in_specs=[VMEM] * 7,
            out_specs=VMEM,
            compiler_params=params(),
            cost_estimate=cost(1, 1),
            name="final",
        )(own_mine, recv, w_own, w_mate, own, mod, arrived[c])
        there = shifted(produced)
        held = [] if handed is None else [handed]
        handed = pl.pallas_call(
            functools.partial(next_kernel, start=starts[c]) if held else first_kernel,
            out_shape=pltpu.HBM((1, rows, width), BF16),
            in_specs=[VMEM] + [HBM] * len(held),
            out_specs=HBM,
            input_output_aliases={1: 0} if held else {},
            scratch_shapes=[pltpu.SemaphoreType.DMA],
            compiler_params=params(),
            cost_estimate=cost(1, 1),
            name="place",
        )(there, *held)
    return handed


def solution(mesh):
    return jax.shard_map(
        body,
        mesh=mesh,
        in_specs=(
            P("section", "sp", None),
            P("section"),
            P("section"),
            P("section", None, None),
            P("section", None, None, "sp"),
            P("section", "sp", None),
            P("section", None, None),
            P("section", None, "sp"),
            P("section", None, "sp"),
        ),
        out_specs=P("section", "sp", None),
        check_vma=False,
    )
```

```python
import functools

import jax
import jax.numpy as jnp
from jax import lax
from jax.experimental import pallas as pl
from jax.experimental.pallas import tpu as pltpu
from jax.sharding import PartitionSpec as P

SHARES = (6, 6, 6, 6)
F32 = jnp.float32
BF16 = jnp.bfloat16
VMEM = pl.BlockSpec(memory_space=pltpu.VMEM)
HBM = pl.BlockSpec(memory_space=pltpu.HBM)
SMEM = pl.BlockSpec(memory_space=pltpu.SMEM)


def params(mib=24):
    return pltpu.CompilerParams(vmem_limit_bytes=int(mib * 1024) * 1024)


def cost(flops, data):
    return pl.CostEstimate(flops=int(flops), bytes_accessed=int(data), transcendentals=0)


def in_hbm(block):
    return pltpu.with_memory_space_constraint(block, pltpu.HBM)


def swapped(block, flip):
    return lax.ppermute(block, "sp", [(i, i ^ flip) for i in range(lax.axis_size("sp"))])


def shifted(block):
    sections = lax.axis_size("section")
    return lax.ppermute(block, "section", [(i, (i + 1) % sections) for i in range(sections)])


def modulated(block, mod):
    width = block.shape[1]
    stream = block.astype(F32)
    mean = jnp.sum(stream, axis=-1, keepdims=True) * (1.0 / width)
    centred = stream - mean
    var = jnp.sum(centred * centred, axis=-1, keepdims=True) * (1.0 / width)
    return (centred * lax.rsqrt(var + 1e-06) * (1.0 + mod[1:2]) + mod[0:1]).astype(BF16)


def head_norm(values, gain):
    size = gain.shape[1]
    heads = []
    for h in range(values.shape[1] // size):
        head = values[:, h * size : (h + 1) * size]
        square = jnp.sum(head * head, axis=-1, keepdims=True) * (1.0 / size)
        heads.append((head * lax.rsqrt(square + 1e-06) * gain).astype(BF16))
    return jnp.concatenate(heads, axis=1)


def qkv(normed, w_ref, gains_ref):
    cols = w_ref.shape[1] // 3
    both = jnp.dot(normed, w_ref[...], preferred_element_type=F32)
    q = head_norm(both[:, :cols], gains_ref[0:1])
    k = head_norm(both[:, cols : 2 * cols], gains_ref[1:2])
    return q, k, both[:, 2 * cols :].astype(BF16)


def attend(q, kt_ref, v_ref, size):
    scale = 1.0 / size**0.5
    heads = []
    for h in range(q.shape[1] // size):
        cols = slice(h * size, (h + 1) * size)
        scores = jnp.dot(q[:, cols], kt_ref[cols, :], preferred_element_type=F32)
        top = jnp.max(scores, axis=-1, keepdims=True)
        weights = jnp.exp((scores - top) * scale)
        total = jnp.sum(weights, axis=-1, keepdims=True)
        out = jnp.dot(weights.astype(BF16), v_ref[:, cols], preferred_element_type=F32)
        heads.append((out / total).astype(BF16))
    return jnp.concatenate(heads, axis=1)


def near_kernel(
    pid_ref, own_hbm, mate_ref, mod_ref, gains_hbm, w_hbm, sk_hbm, sv_hbm, wo_hbm,
    q_ref, kt_ref, v_ref, w_ref, acc_ref, stat_ref, wo_ref,
    xn, own_ref, gains_ref, sk_ref, sems,
):
    rows = own_ref.shape[0]
    size = gains_ref.shape[1]
    heads = q_ref.shape[1] // size
    early = [
        pltpu.make_async_copy(own_hbm, own_ref, sems.at[5]),
        pltpu.make_async_copy(gains_hbm, gains_ref, sems.at[6]),
    ]
    for load in early:
        load.start()
    width = q_ref.shape[1]
    loads = [
        pltpu.make_async_copy(w_hbm.at[i], w_ref.at[:, pl.ds(i * width, width)], sems.at[i])
        for i in range(3)
    ]
    loads.append(pltpu.make_async_copy(sk_hbm, sk_ref, sems.at[3]))
    loads.append(pltpu.make_async_copy(sv_hbm, v_ref, sems.at[4]))
    loads.append(pltpu.make_async_copy(wo_hbm, wo_ref, sems.at[7]))
    loads[3].start()
    loads[0].start()
    loads[1].start()
    xn[rows:] = modulated(mate_ref[...], mod_ref)
    for load in early:
        load.wait()
    xn[:rows] = modulated(own_ref[...], mod_ref)
    first = pl.multiple_of(pid_ref[0] * (4 * rows), 4 * rows)
    loads[3].wait()
    kt_ref[...] = sk_ref[...].T
    loads[0].wait()
    loads[2].start()
    loads[4].start()
    q = head_norm(jnp.dot(xn[...], w_ref[:, :width], preferred_element_type=F32), gains_ref[0:1])
    q_ref[...] = q
    loads[1].wait()
    loads[5].start()
    k = head_norm(jnp.dot(xn[...], w_ref[:, width : 2 * width], preferred_element_type=F32), gains_ref[1:2])
    kt_ref[:, pl.ds(first, 2 * rows)] = k.T
    loads[2].wait()
    v = jnp.dot(xn[...], w_ref[:, 2 * width :], preferred_element_type=F32).astype(BF16)
    loads[4].wait()
    v_ref[pl.ds(first, 2 * rows)] = v
    place = lax.broadcasted_iota(jnp.int32, (1, kt_ref.shape[1]), 1) - (first + 2 * rows)
    bias = jnp.where((place >= 0) & (place < 2 * rows), -1e30, 0.0)
    scale = 1.0 / size**0.5
    for h in range(heads):
        cols = slice(h * size, (h + 1) * size)
        scores = jnp.dot(q[:, cols], kt_ref[cols, :], preferred_element_type=F32) + bias
        top = jnp.max(scores, axis=-1, keepdims=True)
        weights = jnp.exp((scores - top) * scale)
        stat_ref[:, h : h + 1] = top
        stat_ref[:, heads + h : heads + h + 1] = jnp.sum(weights, axis=-1, keepdims=True)
        acc_ref[:, cols] = jnp.dot(weights.astype(BF16), v_ref[:, cols], preferred_element_type=F32)
    loads[5].wait()


def far_kernel(
    pid_ref, own_ref, mate_ref, mod_ref, gains_ref, w_ref, ki_ref, vi_ref, qn_ref, acc_ref, stat_ref,
    q_ref, mine_ref, send_ref, kt_ref, v_ref, xn,
):
    rows = own_ref.shape[0]
    size = gains_ref.shape[1]
    heads = q_ref.shape[1] // size
    scale = 1.0 / size**0.5
    xn[:rows] = modulated(own_ref[...], mod_ref)
    xn[rows:] = modulated(mate_ref[...], mod_ref)
    q, k, v = qkv(xn[...], w_ref, gains_ref)
    first = pl.multiple_of(pid_ref[0] * (4 * rows), 4 * rows) + 2 * rows
    first = pl.multiple_of(first, 2 * rows)
    fresh = k.T
    kt_ref[:, pl.ds(first, 2 * rows)] = fresh
    v_ref[pl.ds(first, 2 * rows)] = v
    q_ref[...] = q[:rows]
    for h in range(heads):
        cols = slice(h * size, (h + 1) * size)
        scores = jnp.dot(qn_ref[:, cols], fresh[cols, :], preferred_element_type=F32)
        before = stat_ref[:, h : h + 1]
        top = jnp.maximum(before, jnp.max(scores, axis=-1, keepdims=True))
        weights = jnp.exp((scores - top) * scale)
        keep = jnp.exp((before - top) * scale)
        total = stat_ref[:, heads + h : heads + h + 1] * keep + jnp.sum(weights, axis=-1, keepdims=True)
        out = acc_ref[:, cols] * keep + jnp.dot(weights.astype(BF16), v[:, cols], preferred_element_type=F32)
        out = (out / total).astype(BF16)
        mine_ref[:, cols] = out[:rows]
        send_ref[:rows, cols] = out[rows:]
    send_ref[rows:] = attend(q[rows:], kt_ref, v_ref, size)


def mine_kernel(q_ref, kt_ref, v_ref, mine_ref, *, size):
    mine_ref[...] = attend(q_ref[...], kt_ref, v_ref, size)


def projected(mine_ref, recv, w_ref, wm_ref, cols):
    part = jnp.dot(mine_ref[...], w_ref[:, cols], preferred_element_type=F32)
    return part + jnp.dot(recv, wm_ref[:, cols], preferred_element_type=F32)


def far_out_kernel(mine_ref, recv_ref, w_ref, wm_ref, *out_refs):
    rows = mine_ref.shape[0]
    start = 0
    for out in out_refs:
        cols = slice(start, start + out.shape[1])
        start = cols.stop
        out[...] = projected(mine_ref, recv_ref[rows:], w_ref, wm_ref, cols).astype(BF16)


def final_kernel(mine_ref, recv_ref, w_ref, wm_ref, stream_ref, mod_ref, far_ref, out_ref, *, start):
    rows = mine_ref.shape[0]
    cols = slice(start, start + out_ref.shape[1])
    part = projected(mine_ref, recv_ref[:rows], w_ref, wm_ref, cols) + far_ref[...].astype(F32)
    out_ref[...] = (stream_ref[:, cols].astype(F32) + mod_ref[2:3, cols] * part).astype(BF16)


def first_kernel(part_ref, out_hbm, sem):
    copy = pltpu.make_async_copy(part_ref, out_hbm.at[0, :, pl.ds(0, part_ref.shape[1])], sem)
    copy.start()
    copy.wait()


def next_kernel(part_ref, held_hbm, out_hbm, sem, *, start):
    copy = pltpu.make_async_copy(part_ref, out_hbm.at[0, :, pl.ds(start, part_ref.shape[1])], sem)
    copy.start()
    copy.wait()


def shape(*dims, dtype=BF16):
    return jax.ShapeDtypeStruct(dims, dtype)


def body(patches, patch_ids, step_ids, modulation, w_qkv, w_out, gains, stale_keys, stale_values):
    rows, width = patches.shape[1:]
    size = gains.shape[2]
    cols = stale_keys.shape[2]
    keys = stale_keys.shape[1]
    own = patches[0]
    x_far = swapped(own, 2)
    x_mate = swapped(own, 1)
    w_mate = swapped(w_out[0], 1)
    mod = lax.dynamic_index_in_dim(modulation[0], step_ids[0], 0, keepdims=False)
    mod = mod.reshape(3, width).astype(F32)
    half_flops = 2 * 2 * rows * width * 3 * cols
    att_flops = 2 * 2 * rows * keys * cols
    q_own, k_part, v_part, w_held, acc, stat, w_own = pl.pallas_call(
        near_kernel,
        out_shape=[
            pltpu.VMEM((2 * rows, cols), BF16),
            pltpu.VMEM((cols, keys), BF16),
            pltpu.VMEM((keys, cols), BF16),
            pltpu.VMEM((width, 3 * cols), BF16),
            pltpu.VMEM((2 * rows, cols), F32),
            pltpu.VMEM((2 * rows, size), F32),
            pltpu.VMEM((cols, width), BF16),
        ],
        in_specs=[SMEM, HBM, VMEM, VMEM] + [HBM] * 5,
        out_specs=[VMEM] * 7,
        scratch_shapes=[
            pltpu.VMEM((2 * rows, width), BF16),
            pltpu.VMEM((rows, width), BF16),
            pltpu.VMEM((2, size), F32),
            pltpu.VMEM((keys, cols), BF16),
            pltpu.SemaphoreType.DMA((8,)),
        ],
        compiler_params=params(),
        cost_estimate=cost(half_flops, 1),
        name="near",
    )(
        patch_ids,
        in_hbm(own),
        x_mate,
        mod,
        in_hbm(gains[0]),
        in_hbm(w_qkv[0]),
        in_hbm(stale_keys[0]),
        in_hbm(stale_values[0]),
        in_hbm(w_out[0]),
    )
    x_far, q_own = lax.optimization_barrier((x_far, q_own))
    x_far_mate = swapped(x_far, 1)
    far_q, own_mine, send, k_all, v_all = pl.pallas_call(
        far_kernel,
        out_shape=[
            pltpu.VMEM((rows, cols), BF16),
            pltpu.VMEM((rows, cols), BF16),
            pltpu.VMEM((2 * rows, cols), BF16),
            pltpu.VMEM((cols, keys), BF16),
            pltpu.VMEM((keys, cols), BF16),
        ],
        in_specs=[SMEM] + [VMEM] * 10,
        out_specs=[VMEM] * 5,
        input_output_aliases={6: 3, 7: 4},
        scratch_shapes=[pltpu.VMEM((2 * rows, width), BF16)],
        compiler_params=params(),
        cost_estimate=cost(half_flops + att_flops, 12e6),
        name="far",
    )(patch_ids, x_far, x_far_mate, mod, gains[0], w_held, k_part, v_part, q_own, acc, stat)
    recv = swapped(send, 1)
    far_mine = pl.pallas_call(
        functools.partial(mine_kernel, size=size),
        out_shape=pltpu.VMEM((rows, cols), BF16),
        in_specs=[VMEM] * 3,
        out_specs=VMEM,
        compiler_params=params(),
        cost_estimate=cost(att_flops, 3e6),
        name="far_mine",
    )(far_q, k_all, v_all)
    recv, far_mine = lax.optimization_barrier((recv, far_mine))
    steps = [width // sum(SHARES) * share for share in SHARES]
    starts = [sum(steps[:c]) for c in range(len(steps))]
    far_parts = pl.pallas_call(
        far_out_kernel,
        out_shape=[pltpu.VMEM((rows, step), BF16) for step in steps],
        in_specs=[VMEM] * 4,
        out_specs=[VMEM] * len(steps),
        compiler_params=params(),
        cost_estimate=cost(2 * rows * 2 * cols * width, 5e6),
        name="far_out",
    )(far_mine, recv, w_own, w_mate)
    far_parts, own_mine = lax.optimization_barrier((far_parts, own_mine))
    arrived = [swapped(part, 2) for part in far_parts]
    handed = produced = None
    for c, step in enumerate(steps):
        if c > 0:
            arrived[c], produced = lax.optimization_barrier((arrived[c], produced))
        produced = pl.pallas_call(
            functools.partial(final_kernel, start=starts[c]),
            out_shape=pltpu.VMEM((rows, step), BF16),
            in_specs=[VMEM] * 7,
            out_specs=VMEM,
            compiler_params=params(),
            cost_estimate=cost(1, 1),
            name="final",
        )(own_mine, recv, w_own, w_mate, own, mod, arrived[c])
        there = shifted(produced)
        held = [] if handed is None else [handed]
        handed = pl.pallas_call(
            functools.partial(next_kernel, start=starts[c]) if held else first_kernel,
            out_shape=pltpu.HBM((1, rows, width), BF16),
            in_specs=[VMEM] + [HBM] * len(held),
            out_specs=HBM,
            input_output_aliases={1: 0} if held else {},
            scratch_shapes=[pltpu.SemaphoreType.DMA],
            compiler_params=params(),
            cost_estimate=cost(1, 1),
            name="place",
        )(there, *held)
    return handed


def solution(mesh):
    return jax.shard_map(
        body,
        mesh=mesh,
        in_specs=(
            P("section", "sp", None),
            P("section"),
            P("section"),
            P("section", None, None),
            P("section", None, None, "sp"),
            P("section", "sp", None),
            P("section", None, None),
            P("section", None, "sp"),
            P("section", None, "sp"),
        ),
        out_specs=P("section", "sp", None),
        check_vma=False,
    )
```
